128 devices in a mesh: ctx: 64 (over z, x, y), tp: 2 (over core).
Axes of the slice: x: 4, y: 4, z: 4, core: 2. Of those that a mesh axis runs over, the one named last changes fastest.
Arguments:
- streams: bfloat16 [32768, 3, 2048], P('ctx', None, 'tp'), may hold values from -6 to 6
- short_filter: float32 [3, 3, 2048], P(None, None, 'tp'), may hold values from -3.5 to 3.5
- long_filter: float32 [32768, 2048], P('ctx', 'tp'), may hold values from -0.03125 to 0.03125
- skip_gain: float32 [2048], P('tp'), may hold values from -4 to 4
- out_weight: bfloat16 [2048, 4096], P('tp'), may hold values from -0.125 to 0.125
Outputs:
- layer_out: bfloat16 [32768, 4096], P('ctx', 'tp')
The draws below stay inside these ranges and needn't reach their ends.
All inputs are finite; a program needn't handle non-finite values.
Results may differ from the reference program's by a relative error of at most 0.0049.
Values may be sent and summed in bfloat16 or wider, within the bound.
A program may use at most 192 MiB of HBM per device.

```python
import jax
import jax.numpy as jnp

D = 4096
C = 2048
TAPS = 3
L = 32768


def steps_of(key, dims, pieces, low, top_value):
    def one(axis_at, shards_of):
        steps = jax.random.uniform(jax.random.fold_in(jax.random.fold_in(key, 6), axis_at), (shards_of,), jnp.float32, low / len(pieces), top_value / len(pieces))
        return jnp.repeat(jnp.exp(steps), dims[axis_at] // shards_of).reshape((-1,) + (1,) * (len(dims) - axis_at - 1))

    loudness = one(*pieces[0])
    for cut in pieces[1:]:
        loudness = loudness * one(*cut)
    return loudness


def gaussian(stream_key, shape, width, bound, shards=(), dtype=jnp.bfloat16):
    factor_of = steps_of(stream_key, shape, shards, -0.22, 0.18) if shards else 1.0
    drawn = jax.random.normal(stream_key, shape, jnp.float32) * width * factor_of
    return jnp.minimum(jnp.maximum(drawn, -bound), bound).astype(dtype)


def setup_inputs(seed: int = 0) -> dict:
    arg_keys = jax.random.split(jax.random.key(seed), 6)
    return {
        "streams": gaussian(arg_keys[0], (L, 3, C), 1.0, 6.0, ((0, 64), (2, 2))),
        "short_filter": gaussian(arg_keys[1], (TAPS, 3, C), TAPS ** -0.5, 3.5, ((2, 2),), jnp.float32),
        "long_filter": gaussian(arg_keys[2], (L, C), L ** -0.5, 0.03125, ((0, 64), (1, 2)), jnp.float32),
        "skip_gain": gaussian(arg_keys[3], (C,), 1.0, 4.0, ((0, 2),), jnp.float32),
        "out_weight": gaussian(arg_keys[4], (C, D), C ** -0.5, 0.125, ((0, 2),)),
    }


def reference(streams, short_filter, long_filter, skip_gain, out_weight):
    length = streams.shape[0]
    widened = streams.astype(jnp.float32)
    zero_rows = jnp.zeros((2,) + widened.shape[1:], jnp.float32)
    padded = jnp.concatenate([zero_rows, widened], axis=0)
    mixed = short_filter[0] * padded[2:] + short_filter[1] * padded[1:-1] + short_filter[2] * padded[:-2]
    gate_side = mixed[:, 0]
    key_side = mixed[:, 1]
    value_side = mixed[:, 2]
    product = key_side * value_side
    doubled = 2 * length
    spectrum = jnp.fft.rfft(product, n=doubled, axis=0) * jnp.fft.rfft(long_filter, n=doubled, axis=0)
    convolved = jnp.fft.irfft(spectrum, n=doubled, axis=0)[:length].astype(jnp.float32)
    gated = (gate_side * (convolved + skip_gain * product)).astype(jnp.bfloat16)
    return jnp.dot(gated, out_weight, preferred_element_type=jnp.float32).astype(jnp.bfloat16)
```

```python
import functools
import itertools
import math

import jax
import jax.numpy as jnp
import ml_dtypes
import numpy as np
from jax import lax
from jax.experimental import pallas as pl
from jax.experimental.pallas import tpu as pltpu
from jax.sharding import PartitionSpec as P

MESH = pl.DeviceIdType.MESH
bf16, f32 = jnp.bfloat16, jnp.float32

PIECES = 2
OWN = 16 // PIECES
PART = 512 // PIECES
LOW = 4 // PIECES
BLOCK = 128 * PIECES
PAIRS = OWN // 2


def split(a):
    high = a.astype(ml_dtypes.bfloat16)
    return high, (a - high.astype(np.float64)).astype(ml_dtypes.bfloat16)


def tables():
    k1 = np.arange(256) + 0.5
    row = np.arange(256)
    angle = 2 * np.pi * np.outer(k1, 4 * (row % 64) + row // 64) / 512
    first = np.concatenate(split(np.concatenate([np.cos(angle), -np.sin(angle)], 0)), 0)
    twist = 2 * np.pi * np.outer(k1, np.arange(128)) / 65536
    twist = np.concatenate([twist, twist], 1)
    inner = 2 * np.pi * (np.outer(np.arange(128), np.arange(128)) % 128) / 128
    c, s = np.cos(inner), np.sin(inner)
    sh, sl = split(np.block([[c, -s], [s, c]]))
    bh, bl = split(np.block([[c, s], [-s, c]]))
    last = np.concatenate(split(np.concatenate([np.cos(angle.T), -np.sin(angle.T)], 1) * (2.0 / 65536)), 0)
    r = np.arange(256)
    swap = np.zeros((256, 256), ml_dtypes.bfloat16)
    swap[r, (r % 16) * 16 + r // 16] = 1
    r = np.arange(BLOCK)
    pick = np.zeros((BLOCK, BLOCK), ml_dtypes.bfloat16)
    pick[r, (r % PIECES) * 128 + r // PIECES] = 1
    return dict(
        first=first,
        tcos=np.cos(twist).astype(np.float32),
        tsin=np.sin(twist).astype(np.float32),
        second=np.concatenate([sh, sh, sl], 0),
        back=np.concatenate([bh, bh, bl], 0),
        last=last,
        swap=swap,
        pick=pick,
        unit=np.eye(PART, dtype=ml_dtypes.bfloat16),
    )


def offsets():
    every = [d for d in itertools.product(range(4), repeat=3) if d != (0, 0, 0)]
    hops = lambda d: sum(min(v, 4 - v) for v in d)
    order = []
    for d in sorted(every, key=lambda d: (-hops(d), (d[0] * 29 + d[1] * 13 + d[2] * 7) % 31)):
        for e in (d, (d[1], d[2], d[0]), (d[2], d[0], d[1])):
            for g in (e, tuple(-v % 4 for v in e)):
                if g not in order:
                    order.append(g)
    return order


def dot(a, b):
    return jnp.dot(a, b, preferred_element_type=f32)


def dot_t(a, b):
    return lax.dot_general(a, b, (((1,), (1,)), ((), ())), preferred_element_type=f32)


def halves(v):
    high = v.astype(bf16)
    return high, (v - high.astype(f32)).astype(bf16)


def at(i, size):
    return pl.ds(pl.multiple_of(i * size, size), size)


def spread(swap, src, base, dst):
    def group(g, carry):
        mixed = dot(swap[...], src[pl.ds(pl.multiple_of(base + g * 256, 256), 256), :]).astype(bf16)
        for c in range(OWN):
            for high in range(PIECES):
                for low in range(LOW):
                    r = c * PIECES + high
                    dst[pl.ds(pl.multiple_of((high * LOW + low) * 64 + g * 16, 16), 16), pl.ds(c * 128, 128)] = mixed[
                        r * 16 : r * 16 + 16, low * 128 : low * 128 + 128
                    ]
        return carry

    lax.fori_loop(0, 4, group, 0)


def gather(swap, src, tmp, dst, base):
    def group(g, carry):
        for c in range(OWN):
            for high in range(PIECES):
                for low in range(LOW):
                    r = c * PIECES + high
                    tmp[pl.ds(r * 16, 16), pl.ds(low * 128, 128)] = src[
                        pl.ds(pl.multiple_of((high * LOW + low) * 64 + g * 16, 16), 16), pl.ds(c * 128, 128)
                    ]
        dst[pl.ds(pl.multiple_of(base + g * 256, 256), 256), :] = dot(swap[...], tmp[...]).astype(bf16)
        return carry

    lax.fori_loop(0, 4, group, 0)


def forward(t, x):
    a = dot(t["first"][...], x)
    re = a[0:256] + a[512:768]
    im = a[256:512] + a[768:1024]
    tc, ts = t["tcos"][...], t["tsin"][...]
    tre = re * tc + im * ts
    tim = im * tc - re * ts
    z = jnp.concatenate(
        [
            jnp.concatenate([tre[:, :128], tim[:, :128]], 1),
            jnp.concatenate([tre[:, 128:], tim[:, 128:]], 1),
        ],
        0,
    )
    zh, zl = halves(z)
    return dot(jnp.concatenate([zh, zl, zh], 1), t["second"][...])


def backward(t, sx, sh):
    xr, xi, hr, hi = sx[:, :128], sx[:, 128:], sh[:, :128], sh[:, 128:]
    yh, yl = halves(jnp.concatenate([xr * hr - xi * hi, xr * hi + xi * hr], 1))
    b = dot(jnp.concatenate([yh, yl, yh], 1), t["back"][...])
    re = jnp.concatenate([b[:256, :128], b[256:, :128]], 1)
    im = jnp.concatenate([b[:256, 128:], b[256:, 128:]], 1)
    tc, ts = t["tcos"][...], t["tsin"][...]
    vh, vl = halves(jnp.concatenate([re * tc - im * ts, im * tc + re * ts], 0))
    o = dot(t["last"][...], vh)
    return (o[:256] + o[256:] + dot(t["last"][:256, :], vl)).astype(bf16)


NAMES = ("first", "tcos", "tsin", "second", "back", "last", "swap", "pick", "unit")


def kernel(*refs):
    n = len(NAMES)
    streams_in, filter_in, weight_in = refs[:3]
    taps, skip = refs[3:5]
    table_in = refs[5 : 5 + n]
    out = refs[5 + n]
    tabs = refs[6 + n : 6 + 2 * n]
    (sv, hv, halo, gate, extra, block, send_h, send_x, send_y, recv_h, recv_x, recv_y) = refs[6 + 2 * n : 18 + 2 * n]
    (xs, spec, ys, tmp, wa, wb, ga, gb, acc) = refs[18 + 2 * n : 27 + 2 * n]
    load_sem, table_sem, link_send, link_recv, pair_send, pair_recv, halo_sem = refs[27 + 2 * n :]
    t = dict(zip(NAMES, tabs))

    me, tp = lax.axis_index("ctx"), lax.axis_index("tp")
    mz, mx, my = me // 16, (me // 4) % 4, me % 4
    order = offsets()

    def peer(d):
        return ((mz + d[0]) % 4) * 16 + ((mx + d[1]) % 4) * 4 + (my + d[2]) % 4

    load_h = pltpu.make_async_copy(filter_in, hv, load_sem.at[0])
    load_s = pltpu.make_async_copy(streams_in, sv, load_sem.at[1])
    load_w = pltpu.make_async_copy(weight_in.at[:, at(tp, 2048)], wa, load_sem.at[2])
    load_t = [pltpu.make_async_copy(a, b, table_sem.at[i]) for i, (a, b) in enumerate(zip(table_in, tabs))]
    load_t[NAMES.index("pick")].start()
    load_h.start()
    load_s.start()

    barrier = pltpu.get_barrier_semaphore()
    for d in order:
        pl.semaphore_signal(barrier, inc=1, device_id=(peer(d), tp), device_id_type=MESH)
    pl.semaphore_signal(barrier, inc=1, device_id=(me, 1 - tp), device_id_type=MESH)

    for i, copy in enumerate(load_t):
        if NAMES[i] != "pick":
            copy.start()
    load_w.start()

    def send(array, src, dst, q):
        for d in order:
            p = peer(d)
            pltpu.make_async_remote_copy(
                src_ref=src.at[pl.ds(pl.multiple_of(q * 1024 + p * 16, 16), 16)],
                dst_ref=dst.at[pl.ds(pl.multiple_of(q * 1024 + me * 16, 16), 16)],
                send_sem=link_send.at[array * PIECES + q],
                recv_sem=link_recv.at[array * PIECES + q],
                device_id=(p, tp),
                device_id_type=MESH,
            ).start()
        mine = pl.ds(pl.multiple_of(q * 1024 + me * 16, 16), 16)
        dst[mine, :] = src[mine, :]

    def arrived(array, buf, q, sem):
        view = buf.at[pl.ds(0, 63 * 16)]
        pltpu.make_async_copy(view, view, sem.at[array * PIECES + q]).wait()

    load_t[NAMES.index("pick")].wait()
    load_h.wait()

    def filter_block(b, carry):
        cols = at(b, 128)
        for part in range(PIECES):
            block[:, pl.ds(part * 128, 128)] = hv[pl.ds(part * PART, PART), cols].astype(bf16)
        send_h[at(b, BLOCK), :] = dot_t(t["pick"][...], block[...]).astype(bf16)
        return carry

    lax.fori_loop(0, 8, filter_block, 0)

    pl.semaphore_wait(barrier, 64)
    after = (me + 1) % 64
    halo_copy = pltpu.make_async_remote_copy(
        src_ref=streams_in.at[:, pl.ds(496, 16), :],
        dst_ref=halo,
        send_sem=halo_sem.at[0],
        recv_sem=halo_sem.at[1],
        device_id=(after, tp),
        device_id_type=MESH,
    )
    halo_copy.start()
    for q in range(PIECES):
        send(0, send_h, recv_h, q)
    weight_copy = pltpu.make_async_remote_copy(
        src_ref=weight_in.at[:, at(1 - tp, 2048)],
        dst_ref=wb,
        send_sem=pair_send.at[PIECES],
        recv_sem=pair_recv.at[PIECES],
        device_id=(me, 1 - tp),
        device_id_type=MESH,
    )
    weight_copy.start()

    load_s.wait()
    halo_copy.wait_recv()

    def product_block(b, carry):
        cols = at(b, 128)
        for r in range(4):
            rows = pl.ds(r * 128, 128)
            sides = []
            for j in range(3):
                if r == 0:
                    before = halo[j, :, cols].astype(f32)
                    before = jnp.where(me > 0, before, jnp.zeros_like(before))
                else:
                    before = sv[j, pl.ds(r * 128 - 16, 16), cols].astype(f32)
                wide = jnp.concatenate([before, sv[j, rows, cols].astype(f32)], 0)
                sides.append(
                    taps[0, pl.ds(j, 1), cols] * wide[16:]
                    + taps[1, pl.ds(j, 1), cols] * pltpu.roll(wide, 1, 0)[16:]
                    + taps[2, pl.ds(j, 1), cols] * pltpu.roll(wide, 2, 0)[16:]
                )
            product = sides[1] * sides[2]
            gate[rows, cols] = sides[0]
            extra[rows, cols] = skip[:, cols] * product
            part = r * 128 // PART
            block[pl.ds(r * 128 - part * PART, 128), pl.ds(part * 128, 128)] = product.astype(bf16)
        send_x[at(b, BLOCK), :] = dot_t(t["pick"][...], block[...]).astype(bf16)
        return carry

    for q in range(PIECES):
        lax.fori_loop(q * (8 // PIECES), (q + 1) * (8 // PIECES), product_block, 0)
        send(1, send_x, recv_x, q)

    for i, copy in enumerate(load_t):
        if NAMES[i] != "pick":
            copy.wait()

    for q in range(PIECES):
        arrived(0, recv_h, q, link_recv)
        spread(t["swap"], recv_h, q * 1024, xs)

        def filter_pair(j, carry):
            spec[q * PAIRS + j] = forward(t, xs[:, at(j, 256)])
            return carry

        lax.fori_loop(0, PAIRS, filter_pair, 0)

    for q in range(PIECES):
        arrived(1, recv_x, q, link_recv)
        spread(t["swap"], recv_x, q * 1024, xs)

        def product_pair(j, carry):
            ys[:, at(j, 256)] = backward(t, forward(t, xs[:, at(j, 256)]), spec[q * PAIRS + j])
            return carry

        lax.fori_loop(0, PAIRS, product_pair, 0)
        gather(t["swap"], ys, tmp, send_y, q * 1024)
        send(2, send_y, recv_y, q)

    load_w.wait()
    width = 1024 // PIECES
    for q in range(PIECES):
        arrived(2, recv_y, q, link_recv)

        def gate_block(b, carry):
            turned = dot_t(t["unit"][...], recv_y[at(b, BLOCK), :]).astype(bf16)
            conv = dot(turned, t["pick"][...])
            for part in range(PIECES):
                rows, cols = pl.ds(part * PART, PART), at(b, 128)
                ga[rows, cols] = (gate[rows, cols] * (conv[:, part * 128 : part * 128 + 128] + extra[rows, cols])).astype(bf16)
            return carry

        lax.fori_loop(q * (8 // PIECES), (q + 1) * (8 // PIECES), gate_block, 0)
        chans = pl.ds(q * width, width)
        pair_copy = pltpu.make_async_remote_copy(
            src_ref=ga.at[:, chans],
            dst_ref=gb.at[:, chans],
            send_sem=pair_send.at[q],
            recv_sem=pair_recv.at[q],
            device_id=(me, 1 - tp),
            device_id_type=MESH,
        )
        pair_copy.start()

        def own_part(i, carry):
            cols = at(i, 256)
            term = dot(ga[:, chans], wa[chans, cols])
            acc[:, cols] = term if q == 0 else acc[:, cols] + term
            return carry

        lax.fori_loop(0, 8, own_part, 0)
        if q == 0:
            weight_copy.wait()
        pair_copy.wait()

        def other_part(i, carry):
            cols = at(i, 256)
            total = acc[:, cols] + dot(gb[:, chans], wb[chans, cols])
            if q == PIECES - 1:
                out[:, cols] = total.astype(bf16)
            else:
                acc[:, cols] = total
            return carry

        lax.fori_loop(0, 8, other_part, 0)

    halo_copy.wait_send()
    for array, buf in ((0, send_h), (1, send_x), (2, send_y)):
        for q in range(PIECES):
            arrived(array, buf, q, link_send)


def body(streams, short_filter, long_filter, skip_gain, out_weight):
    consts = tables()
    consts = [jnp.asarray(consts[name]) for name in NAMES]
    hbm = pl.BlockSpec(memory_space=pl.ANY)
    vmem = pl.BlockSpec(memory_space=pltpu.VMEM)
    links = lambda: pltpu.VMEM((PIECES * 1024, PART), bf16)
    dma = pltpu.SemaphoreType.DMA
    return pl.pallas_call(
        kernel,
        out_shape=jax.ShapeDtypeStruct((512, 2048), bf16),
        in_specs=[hbm, hbm, hbm, vmem, vmem] + [hbm] * len(NAMES),
        out_specs=vmem,
        scratch_shapes=[pltpu.VMEM(c.shape, c.dtype) for c in consts]
        + [
            pltpu.VMEM((3, 512, 1024), bf16),
            pltpu.VMEM((512, 1024), f32),
            pltpu.VMEM((3, 16, 1024), bf16),
            pltpu.VMEM((512, 1024), f32),
            pltpu.VMEM((512, 1024), f32),
            pltpu.VMEM((PART, BLOCK), bf16),
            links(),
            links(),
            links(),
            links(),
            links(),
            links(),
            pltpu.VMEM((256, OWN * 128), bf16),
            pltpu.VMEM((8, 512, 256), f32),
            pltpu.VMEM((256, OWN * 128), bf16),
            pltpu.VMEM((256, LOW * 128), bf16),
            pltpu.VMEM((1024, 2048), bf16),
            pltpu.VMEM((1024, 2048), bf16),
            pltpu.VMEM((512, 1024), bf16),
            pltpu.VMEM((512, 1024), bf16),
            pltpu.VMEM((512, 2048), f32),
            dma((3,)),
            dma((len(NAMES),)),
            dma((3 * PIECES,)),
            dma((3 * PIECES,)),
            dma((PIECES + 1,)),
            dma((PIECES + 1,)),
            dma((2,)),
        ],
        compiler_params=pltpu.CompilerParams(collective_id=0, has_side_effects=True, vmem_limit_bytes=60 << 20),
        name="hyena",
    )(jnp.transpose(streams, (1, 0, 2)), long_filter, out_weight, short_filter, skip_gain[None, :], *consts)


def solution(mesh):
    return jax.shard_map(
        body,
        mesh=mesh,
        in_specs=(
            P("ctx", None, "tp"),
            P(None, None, "tp"),
            P("ctx", "tp"),
            P("tp"),
            P("tp", None),
        ),
        out_specs=P("ctx", "tp"),
        check_vma=False,
    )
```

```python
import functools
import itertools
import random

import jax
import jax.numpy as jnp
import ml_dtypes
import numpy as np
from jax import lax
from jax.experimental import pallas as pl
from jax.experimental.pallas import tpu as pltpu
from jax.sharding import PartitionSpec as P

MESH = pl.DeviceIdType.MESH
bf16, f32 = jnp.bfloat16, jnp.float32

PIECES = 4
OWN = 16 // PIECES
PART = 512 // PIECES
BLOCK = 128 * PIECES
WIDTH = 1024 // PIECES


def split(a):
    high = a.astype(ml_dtypes.bfloat16)
    return high, (a - high.astype(np.float64)).astype(ml_dtypes.bfloat16)


def tables():
    k1 = np.arange(256) + 0.5
    row = np.arange(256)
    angle = 2 * np.pi * np.outer(k1, 4 * (row % 64) + row // 64) / 512
    first = np.concatenate(split(np.concatenate([np.cos(angle), -np.sin(angle)], 0)), 0)
    twist = 2 * np.pi * np.outer(k1, np.arange(128)) / 65536
    inner = 2 * np.pi * (np.outer(np.arange(128), np.arange(128)) % 128) / 128
    c, s = np.cos(inner), np.sin(inner)
    sh, sl = split(np.block([[c, -s], [s, c]]))
    bh, bl = split(np.block([[c, s], [-s, c]]))
    last = np.concatenate(split(np.concatenate([np.cos(angle.T), -np.sin(angle.T)], 1) * (2.0 / 65536)), 0)
    r = np.arange(256)
    swap = np.zeros((256, 256), ml_dtypes.bfloat16)
    swap[r, (r % 16) * 16 + r // 16] = 1
    r = np.arange(BLOCK)
    pick = np.zeros((BLOCK, BLOCK), ml_dtypes.bfloat16)
    pick[r, (r % PIECES) * 128 + r // PIECES] = 1
    return dict(
        first=first,
        tcos=np.cos(twist).astype(np.float32),
        tsin=np.sin(twist).astype(np.float32),
        second=np.concatenate([sh, sh, sl], 0),
        back=np.concatenate([bh, bh, bl], 0),
        last=last,
        swap=swap,
        pick=pick,
        unit=np.eye(PART, dtype=ml_dtypes.bfloat16),
    )


def offsets():
    every = [d for d in itertools.product(range(4), repeat=3) if d != (0, 0, 0)]
    random.Random(1).shuffle(every)
    order = []
    for d in sorted(every, key=lambda d: -sum(min(v, 4 - v) for v in d)):
        for e in (d, (d[1], d[2], d[0]), (d[2], d[0], d[1])):
            for g in (e, tuple(-v % 4 for v in e)):
                if g not in order:
                    order.append(g)
    return order


def dot(a, b):
    return jnp.dot(a, b, preferred_element_type=f32)


def dot_t(a, b):
    return lax.dot_general(a, b, (((1,), (1,)), ((), ())), preferred_element_type=f32)


def halves(v):
    high = v.astype(bf16)
    return high, (v - high.astype(f32)).astype(bf16)


def at(i, size):
    return pl.ds(pl.multiple_of(i * size, size), size)


def stack(tiles, rows, columns):
    return jnp.concatenate([jnp.concatenate([tiles(r, c) for r in range(rows)], 0) for c in range(columns)], 1)


def spread(swap, src, q):
    rows = jnp.concatenate([src[pl.ds(pl.multiple_of(q * 1024 + g * 256, 256), 256), :] for g in range(4)], 1)
    mixed = dot(swap[...], rows).astype(bf16)

    def tile(r, c):
        part, g = r // 4, r % 4
        low = (c * PIECES + part) * 16
        return mixed[low : low + 16, g * 128 : g * 128 + 128]

    return stack(tile, 16, OWN)


def gather(swap, y, dst, q):
    def tile(r, g):
        c, part = r // PIECES, r % PIECES
        low = part * 64 + g * 16
        return y[low : low + 16, c * 128 : c * 128 + 128]

    mixed = dot(swap[...], stack(tile, 16, 4)).astype(bf16)
    for g in range(4):
        dst[pl.ds(pl.multiple_of(q * 1024 + g * 256, 256), 256), :] = mixed[:, g * 128 : g * 128 + 128]


def forward(t, x):
    a = dot(t["first"][...], x)
    re = a[0:256] + a[512:768]
    im = a[256:512] + a[768:1024]
    tc, ts = t["tcos"][...], t["tsin"][...]
    parts = []
    for c in range(OWN):
        r, i = re[:, c * 128 : c * 128 + 128], im[:, c * 128 : c * 128 + 128]
        parts.append(jnp.concatenate([r * tc + i * ts, i * tc - r * ts], 1))
    zh, zl = halves(jnp.concatenate(parts, 0))
    return dot(jnp.concatenate([zh, zl, zh], 1), t["second"][...])


def backward(t, sx, sh):
    xr, xi, hr, hi = sx[:, :128], sx[:, 128:], sh[:, :128], sh[:, 128:]
    yh, yl = halves(jnp.concatenate([xr * hr - xi * hi, xr * hi + xi * hr], 1))
    b = dot(jnp.concatenate([yh, yl, yh], 1), t["back"][...])
    tc, ts = t["tcos"][...], t["tsin"][...]
    res, ims = [], []
    for c in range(OWN):
        r, i = b[c * 256 : c * 256 + 256, :128], b[c * 256 : c * 256 + 256, 128:]
        res.append(r * tc - i * ts)
        ims.append(i * tc + r * ts)
    vh, vl = halves(jnp.concatenate([jnp.concatenate(res, 1), jnp.concatenate(ims, 1)], 0))
    o = dot(t["last"][...], vh)
    return (o[:256] + o[256:] + dot(t["last"][:256, :], vl)).astype(bf16)


NAMES = ("first", "tcos", "tsin", "second", "back", "last", "swap", "pick", "unit")


def kernel(*refs):
    n = len(NAMES)
    streams_in, filter_in, weight_in = refs[:3]
    taps, skip = refs[3:5]
    table_in = refs[5 : 5 + n]
    out = refs[5 + n]
    tabs = refs[6 + n : 6 + 2 * n]
    (sv, hv, halo, gate, extra, block, send_h, send_x, send_y, recv_h, recv_x, recv_y) = refs[6 + 2 * n : 18 + 2 * n]
    (spec, wa, wb, ga, gb, acc, done) = refs[18 + 2 * n : 25 + 2 * n]
    load_sem, table_sem, link_send, link_recv, pair_send, pair_recv, halo_sem, out_sem = refs[25 + 2 * n :]
    t = dict(zip(NAMES, tabs))

    me, tp = lax.axis_index("ctx"), lax.axis_index("tp")
    mz, mx, my = me // 16, (me // 4) % 4, me % 4
    order = offsets()

    def peer(d):
        return ((mz + d[0]) % 4) * 16 + ((mx + d[1]) % 4) * 4 + (my + d[2]) % 4

    load_h = pltpu.make_async_copy(filter_in, hv, load_sem.at[0])
    load_s = pltpu.make_async_copy(streams_in, sv, load_sem.at[1])
    load_w = pltpu.make_async_copy(weight_in.at[:, at(tp, 2048)], wa, load_sem.at[2])
    load_t = [pltpu.make_async_copy(a, b, table_sem.at[i]) for i, (a, b) in enumerate(zip(table_in, tabs))]
    load_t[NAMES.index("pick")].start()
    load_h.start()
    load_s.start()

    barrier = pltpu.get_barrier_semaphore()
    for d in order:
        pl.semaphore_signal(barrier, inc=1, device_id=(peer(d), tp), device_id_type=MESH)
    pl.semaphore_signal(barrier, inc=1, device_id=(me, 1 - tp), device_id_type=MESH)

    for i, copy in enumerate(load_t):
        if NAMES[i] != "pick":
            copy.start()
    load_w.start()

    def send(array, src, dst, q):
        for d in order:
            p = peer(d)
            pltpu.make_async_remote_copy(
                src_ref=src.at[pl.ds(pl.multiple_of(q * 1024 + p * 16, 16), 16)],
                dst_ref=dst.at[pl.ds(pl.multiple_of(q * 1024 + me * 16, 16), 16)],
                send_sem=link_send.at[array * PIECES + q],
                recv_sem=link_recv.at[array * PIECES + q],
                device_id=(p, tp),
                device_id_type=MESH,
            ).start()
        mine = pl.ds(pl.multiple_of(q * 1024 + me * 16, 16), 16)
        dst[mine, :] = src[mine, :]

    def arrived(array, buf, q, sem):
        view = buf.at[pl.ds(0, 63 * 16)]
        pltpu.make_async_copy(view, view, sem.at[array * PIECES + q]).wait()

    load_t[NAMES.index("pick")].wait()
    load_h.wait()

    def filter_block(b, carry):
        cols = at(b, 128)
        for part in range(PIECES):
            block[:, pl.ds(part * 128, 128)] = hv[pl.ds(part * PART, PART), cols].astype(bf16)
        send_h[at(b, BLOCK), :] = dot_t(t["pick"][...], block[...]).astype(bf16)
        return carry

    lax.fori_loop(0, 8, filter_block, 0)

    pl.semaphore_wait(barrier, 64)
    after = (me + 1) % 64
    halo_copy = pltpu.make_async_remote_copy(
        src_ref=streams_in.at[:, pl.ds(496, 16), :],
        dst_ref=halo,
        send_sem=halo_sem.at[0],
        recv_sem=halo_sem.at[1],
        device_id=(after, tp),
        device_id_type=MESH,
    )
    halo_copy.start()

    def send_filter(q, carry):
        send(0, send_h, recv_h, q)
        return carry

    lax.fori_loop(0, PIECES, send_filter, 0)
    weight_copy = pltpu.make_async_remote_copy(
        src_ref=weight_in.at[:, at(1 - tp, 2048)],
        dst_ref=wb,
        send_sem=pair_send.at[PIECES],
        recv_sem=pair_recv.at[PIECES],
        device_id=(me, 1 - tp),
        device_id_type=MESH,
    )
    weight_copy.start()

    load_s.wait()
    halo_copy.wait_recv()

    def product_block(b, carry):
        cols = at(b, 128)
        for r in range(4):
            rows = pl.ds(r * 128, 128)
            sides = []
            for j in range(3):
                if r == 0:
                    before = halo[j, :, cols].astype(f32)
                    before = jnp.where(me > 0, before, jnp.zeros_like(before))
                else:
                    before = sv[j, pl.ds(r * 128 - 16, 16), cols].astype(f32)
                wide = jnp.concatenate([before, sv[j, rows, cols].astype(f32)], 0)
                sides.append(
                    taps[0, pl.ds(j, 1), cols] * wide[16:]
                    + taps[1, pl.ds(j, 1), cols] * pltpu.roll(wide, 1, 0)[16:]
                    + taps[2, pl.ds(j, 1), cols] * pltpu.roll(wide, 2, 0)[16:]
                )
            product = sides[1] * sides[2]
            gate[rows, cols] = sides[0]
            extra[rows, cols] = skip[:, cols] * product
            part = r * 128 // PART
            block[pl.ds(r * 128 - part * PART, 128), pl.ds(part * 128, 128)] = product.astype(bf16)
        send_x[at(b, BLOCK), :] = dot_t(t["pick"][...], block[...]).astype(bf16)
        return carry

    def send_product(q, carry):
        lax.fori_loop(q * (8 // PIECES), (q + 1) * (8 // PIECES), product_block, 0)
        send(1, send_x, recv_x, q)
        return carry

    lax.fori_loop(0, PIECES, send_product, 0)

    for i, copy in enumerate(load_t):
        if NAMES[i] != "pick":
            copy.wait()

    def filter_piece(q, carry):
        arrived(0, recv_h, q, link_recv)
        spec[q] = forward(t, spread(t["swap"], recv_h, q))
        return carry

    lax.fori_loop(0, PIECES, filter_piece, 0)

    def product_piece(q, carry):
        arrived(1, recv_x, q, link_recv)
        y = backward(t, forward(t, spread(t["swap"], recv_x, q)), spec[q])
        gather(t["swap"], y, send_y, q)
        send(2, send_y, recv_y, q)
        return carry

    lax.fori_loop(0, PIECES, product_piece, 0)

    load_w.wait()
    weight_copy.wait()
    copies = []
    for q in range(PIECES):
        arrived(2, recv_y, q, link_recv)

        def gate_block(b, carry):
            turned = dot_t(t["unit"][...], recv_y[at(b, BLOCK), :]).astype(bf16)
            conv = dot(turned, t["pick"][...])
            for part in range(PIECES):
                rows, cols = pl.ds(part * PART, PART), at(b, 128)
                ga[rows, cols] = (gate[rows, cols] * (conv[:, part * 128 : part * 128 + 128] + extra[rows, cols])).astype(bf16)
            return carry

        lax.fori_loop(q * (8 // PIECES), (q + 1) * (8 // PIECES), gate_block, 0)
        chans = pl.ds(q * WIDTH, WIDTH)
        copies.append(
            pltpu.make_async_remote_copy(
                src_ref=ga.at[:, chans],
                dst_ref=gb.at[:, chans],
                send_sem=pair_send.at[q],
                recv_sem=pair_recv.at[q],
                device_id=(me, 1 - tp),
                device_id_type=MESH,
            )
        )
        copies[q].start()
        if q > 0:
            copies[q - 1].wait()

        def project(i, carry):
            cols = at(i, 256)
            left, right = ga[:, chans], wa[chans, cols]
            if q == 0:
                acc[:, cols] = dot(left, right)
            else:
                before = pl.ds((q - 1) * WIDTH, WIDTH)
                left = jnp.concatenate([left, gb[:, before]], 1)
                right = jnp.concatenate([right, wb[before, cols]], 0)
                acc[:, cols] = acc[:, cols] + dot(left, right)
            return carry

        lax.fori_loop(0, 8, project, 0)

    copies[-1].wait()

    def out_copy(i):
        return pltpu.make_async_copy(done.at[:, at(i, 512)], out.at[:, at(i, 512)], out_sem.at[i])

    def finish(i, carry):
        for half in range(2):
            cols = at(2 * i + half, 256)
            final = pl.ds((PIECES - 1) * WIDTH, WIDTH)
            done[:, cols] = (acc[:, cols] + dot(gb[:, final], wb[final, cols])).astype(bf16)
        out_copy(i).start()
        return carry

    lax.fori_loop(0, 4, finish, 0)
    for i in range(4):
        out_copy(i).wait()
    halo_copy.wait_send()
    for array, buf in ((0, send_h), (1, send_x), (2, send_y)):
        for q in range(PIECES):
            arrived(array, buf, q, link_send)


def handed_on(src, dst, held, sem):
    rows = [pl.ds(i * 128, 128) for i in range(4)]
    reads = [pltpu.make_async_copy(src.at[r], held.at[r], sem.at[0, i]) for i, r in enumerate(rows)]
    writes = [pltpu.make_async_copy(held.at[r], dst.at[r], sem.at[1, i]) for i, r in enumerate(rows)]
    for copy in reads:
        copy.start()
    for i in range(4):
        reads[i].wait()
        writes[i].start()
    for copy in writes:
        copy.wait()


def body(streams, short_filter, long_filter, skip_gain, out_weight):
    consts = tables()
    consts = [jnp.asarray(consts[name]) for name in NAMES]
    hbm = pl.BlockSpec(memory_space=pl.ANY)
    vmem = pl.BlockSpec(memory_space=pltpu.VMEM)
    links = lambda: pltpu.VMEM((PIECES * 1024, PART), bf16)
    dma = pltpu.SemaphoreType.DMA
    result = pl.pallas_call(
        kernel,
        out_shape=jax.ShapeDtypeStruct((512, 2048), bf16),
        in_specs=[hbm, hbm, hbm, vmem, vmem] + [hbm] * len(NAMES),
        out_specs=hbm,
        scratch_shapes=[pltpu.VMEM(c.shape, c.dtype) for c in consts]
        + [
            pltpu.VMEM((3, 512, 1024), bf16),
            pltpu.VMEM((512, 1024), f32),
            pltpu.VMEM((3, 16, 1024), bf16),
            pltpu.VMEM((512, 1024), f32),
            pltpu.VMEM((512, 1024), f32),
            pltpu.VMEM((PART, BLOCK), bf16),
            links(),
            links(),
            links(),
            links(),
            links(),
            links(),
            pltpu.VMEM((PIECES, OWN * 256, 256), f32),
            pltpu.VMEM((1024, 2048), bf16),
            pltpu.VMEM((1024, 2048), bf16),
            pltpu.VMEM((512, 1024), bf16),
            pltpu.VMEM((512, 1024), bf16),
            pltpu.VMEM((512, 2048), f32),
            pltpu.VMEM((512, 2048), bf16),
            dma((3,)),
            dma((len(NAMES),)),
            dma((3 * PIECES,)),
            dma((3 * PIECES,)),
            dma((PIECES + 1,)),
            dma((PIECES + 1,)),
            dma((2,)),
            dma((4,)),
        ],
        compiler_params=pltpu.CompilerParams(collective_id=0, has_side_effects=True, vmem_limit_bytes=60 << 20),
        name="hyena",
    )(jnp.transpose(streams, (1, 0, 2)), long_filter, out_weight, short_filter, skip_gain[None, :], *consts)
    return pl.pallas_call(
        handed_on,
        out_shape=jax.ShapeDtypeStruct((512, 2048), bf16),
        in_specs=[hbm],
        out_specs=hbm,
        scratch_shapes=[pltpu.VMEM((512, 2048), bf16), dma((2, 4))],
        name="handed_on",
    )(result)


def solution(mesh):
    return jax.shard_map(
        body,
        mesh=mesh,
        in_specs=(
            P("ctx", None, "tp"),
            P(None, None, "tp"),
            P("ctx", "tp"),
            P("tp"),
            P("tp", None),
        ),
        out_specs=P("ctx", "tp"),
        check_vma=False,
    )
```

```python
import functools
import itertools
import random

import jax
import jax.numpy as jnp
import ml_dtypes
import numpy as np
from jax import lax
from jax.experimental import pallas as pl
from jax.experimental.pallas import tpu as pltpu
from jax.sharding import PartitionSpec as P

MESH = pl.DeviceIdType.MESH
bf16, f32 = jnp.bfloat16, jnp.float32

PIECES = 4
OWN = 16 // PIECES
PART = 512 // PIECES
BLOCK = 128 * PIECES
WIDTH = 1024 // PIECES
STEPS = (2, 2, 2)


def split(a):
    high = a.astype(ml_dtypes.bfloat16)
    return high, (a - high.astype(np.float64)).astype(ml_dtypes.bfloat16)


def tables():
    k1 = np.arange(256) + 0.5
    row = np.arange(256)
    angle = 2 * np.pi * np.outer(k1, 4 * (row % 64) + row // 64) / 512
    first = np.concatenate(split(np.concatenate([np.cos(angle), -np.sin(angle)], 0)), 0)
    twist = 2 * np.pi * np.outer(k1, np.arange(128)) / 65536
    inner = 2 * np.pi * (np.outer(np.arange(128), np.arange(128)) % 128) / 128
    c, s = np.cos(inner), np.sin(inner)
    sh, sl = split(np.block([[c, -s], [s, c]]))
    bh, bl = split(np.block([[c, s], [-s, c]]))
    last = np.concatenate(split(np.concatenate([np.cos(angle.T), -np.sin(angle.T)], 1) * (2.0 / 65536)), 0)
    r = np.arange(256)
    swap = np.zeros((256, 256), ml_dtypes.bfloat16)
    swap[r, (r % 16) * 16 + r // 16] = 1
    r = np.arange(BLOCK)
    pick = np.zeros((BLOCK, BLOCK), ml_dtypes.bfloat16)
    pick[r, (r % PIECES) * 128 + r // PIECES] = 1
    return dict(
        first=first,
        tcos=np.cos(twist).astype(np.float32),
        tsin=np.sin(twist).astype(np.float32),
        second=np.concatenate([sh, sh, sl], 0),
        back=np.concatenate([bh, bh, bl], 0),
        last=last,
        swap=swap,
        pick=pick,
    )


def offsets():
    every = [d for d in itertools.product(range(4), repeat=3) if d != (0, 0, 0)]
    random.Random(1).shuffle(every)
    order = []
    for d in sorted(every, key=lambda d: -sum(min(v, 4 - v) for v in d)):
        for e in (d, (d[1], d[2], d[0]), (d[2], d[0], d[1])):
            for g in (e, tuple(-v % 4 for v in e)):
                if g not in order:
                    order.append(g)
    return order


def dot(a, b):
    return jnp.dot(a, b, preferred_element_type=f32)


def dot_t(a, b):
    return lax.dot_general(a, b, (((1,), (1,)), ((), ())), preferred_element_type=f32)


def halves(v):
    high = v.astype(bf16)
    return high, (v - high.astype(f32)).astype(bf16)


def at(i, size):
    return pl.ds(pl.multiple_of(i * size, size), size)


def stack(tiles, rows, columns):
    return jnp.concatenate([jnp.concatenate([tiles(r, c) for r in range(rows)], 0) for c in range(columns)], 1)


def place(q, step):
    return (q // step) * 1024, (q % step) * 128


def spread(swap, src, row, lane):
    rows = jnp.concatenate(
        [src[pl.ds(pl.multiple_of(row + g * 256, 256), 256), pl.ds(lane, 128)] for g in range(4)], 1
    )
    mixed = dot(swap[...], rows).astype(bf16)

    def tile(r, c):
        part, g = r // 4, r % 4
        low = (c * PIECES + part) * 16
        return mixed[low : low + 16, g * 128 : g * 128 + 128]

    return stack(tile, 16, OWN)


def gather(swap, y, dst, row, lane):
    def tile(r, g):
        c, part = r // PIECES, r % PIECES
        low = part * 64 + g * 16
        return y[low : low + 16, c * 128 : c * 128 + 128]

    mixed = dot(swap[...], stack(tile, 16, 4)).astype(bf16)
    for g in range(4):
        dst[pl.ds(pl.multiple_of(row + g * 256, 256), 256), pl.ds(lane, 128)] = mixed[:, g * 128 : g * 128 + 128]


def forward(t, x):
    a = dot(t["first"][...], x)
    re = a[0:256] + a[512:768]
    im = a[256:512] + a[768:1024]
    tc, ts = t["tcos"][...], t["tsin"][...]
    parts = []
    for c in range(OWN):
        r, i = re[:, c * 128 : c * 128 + 128], im[:, c * 128 : c * 128 + 128]
        parts.append(jnp.concatenate([r * tc + i * ts, i * tc - r * ts], 1))
    zh, zl = halves(jnp.concatenate(parts, 0))
    return dot(jnp.concatenate([zh, zl, zh], 1), t["second"][...])


def backward(t, sx, sh, count):
    xr, xi, hr, hi = sx[:, :128], sx[:, 128:], sh[:, :128], sh[:, 128:]
    yh, yl = halves(jnp.concatenate([xr * hr - xi * hi, xr * hi + xi * hr], 1))
    b = dot(jnp.concatenate([yh, yl, yh], 1), t["back"][...])
    tc, ts = t["tcos"][...], t["tsin"][...]
    res, ims = [], []
    for c in range(count):
        r, i = b[c * 256 : c * 256 + 256, :128], b[c * 256 : c * 256 + 256, 128:]
        res.append(r * tc - i * ts)
        ims.append(i * tc + r * ts)
    vh, vl = halves(jnp.concatenate([jnp.concatenate(res, 1), jnp.concatenate(ims, 1)], 0))
    o = dot(t["last"][...], vh)
    return (o[:256] + o[256:] + dot(t["last"][:256, :], vl)).astype(bf16)


NAMES = ("first", "tcos", "tsin", "second", "back", "last", "swap", "pick")


def kernel(*refs):
    n = len(NAMES)
    streams_in, filter_in, weight_in = refs[:3]
    taps, skip = refs[3:5]
    table_in = refs[5 : 5 + n]
    out = refs[5 + n]
    tabs = refs[6 + n : 6 + 2 * n]
    (sv, hv, tail, halo, gate, extra, send_h, send_x, send_y, recv_h, recv_x, recv_y) = refs[6 + 2 * n : 18 + 2 * n]
    (xs, sx, ys, spec, wa, wb, ga, gb, acc, done) = refs[18 + 2 * n : 28 + 2 * n]
    load_sem, table_sem, link_send, link_recv, pair_send, pair_recv, halo_sem, out_sem = refs[28 + 2 * n :]
    t = dict(zip(NAMES, tabs))

    me, tp = lax.axis_index("ctx"), lax.axis_index("tp")
    mz, mx, my = me // 16, lax.rem(me // 4, 4), lax.rem(me, 4)
    along = [[lax.rem(m + i, 4) * scale for i in range(4)] for m, scale in ((mz, 16), (mx, 4), (my, 1))]
    order = offsets()

    def peer(d):
        return along[0][d[0]] + along[1][d[1]] + along[2][d[2]]

    load_h = pltpu.make_async_copy(filter_in, hv, load_sem.at[0])
    load_s = pltpu.make_async_copy(streams_in, sv, load_sem.at[1])
    load_w = pltpu.make_async_copy(weight_in.at[:, at(tp, 2048)], wa, load_sem.at[2])
    load_t = [pltpu.make_async_copy(a, b, table_sem.at[i]) for i, (a, b) in enumerate(zip(table_in, tabs))]
    load_t[NAMES.index("pick")].start()
    load_h.start()
    load_s.start()

    barrier = pltpu.get_barrier_semaphore()
    for d in order:
        pl.semaphore_signal(barrier, inc=1, device_id=(peer(d), tp), device_id_type=MESH)
    pl.semaphore_signal(barrier, inc=1, device_id=(me, 1 - tp), device_id_type=MESH)

    for i, copy in enumerate(load_t):
        if NAMES[i] != "pick":
            copy.start()
    load_w.start()

    def send(array, src, dst, q):
        base = (q // STEPS[array]) * 1024
        for d in order:
            p = peer(d)
            pltpu.make_async_remote_copy(
                src_ref=src.at[pl.ds(pl.multiple_of(base + p * 16, 16), 16)],
                dst_ref=dst.at[pl.ds(pl.multiple_of(base + me * 16, 16), 16)],
                send_sem=link_send.at[array * PIECES + q],
                recv_sem=link_recv.at[array * PIECES + q],
                device_id=(p, tp),
                device_id_type=MESH,
            ).start()
        mine = pl.ds(pl.multiple_of(base + me * 16, 16), 16)
        dst[mine, :] = src[mine, :]

    def arrived(array, buf, q, sem):
        view = buf.at[pl.ds(0, 63 * 16)]
        pltpu.make_async_copy(view, view, sem.at[array * PIECES + q]).wait()

    def block_at(array, b):
        row, lane = place(b // 2, STEPS[array])
        return pl.ds(pl.multiple_of(row + (b % 2) * BLOCK, BLOCK), BLOCK), pl.ds(pl.multiple_of(lane, 128), 128)

    load_t[NAMES.index("pick")].wait()
    load_h.wait()

    def filter_block(b, carry):
        parts = [hv[pl.ds(part * PART, PART), at(b, 128)].astype(bf16) for part in range(PIECES)]
        send_h[block_at(0, b)] = dot_t(t["pick"][...], jnp.concatenate(parts, 1)).astype(bf16)
        return carry

    lax.fori_loop(0, 8, filter_block, 0, unroll=4)

    load_s.wait()
    line = lax.broadcasted_iota(jnp.int32, (16, 1024), 0)
    packed = jnp.zeros((16, 1024), f32)
    for j in range(3):
        rows = pltpu.roll(sv[j, pl.ds(496, 16), :].astype(f32), 2 + 2 * j, 0)
        packed = jnp.where((line >= 2 * j) & (line < 2 * j + 2), rows, packed)
    tail[...] = packed.astype(bf16)

    pl.semaphore_wait(barrier, 64)
    after = lax.rem(me + 1, 64)
    for i in range(4):
        pltpu.make_async_remote_copy(
            src_ref=tail.at[:, pl.ds(i * 256, 256)],
            dst_ref=halo.at[:, pl.ds(i * 256, 256)],
            send_sem=halo_sem.at[0],
            recv_sem=halo_sem.at[1],
            device_id=(after, tp),
            device_id_type=MESH,
        ).start()
    for q in range(0, PIECES, STEPS[0]):
        send(0, send_h, recv_h, q)
    pltpu.make_async_copy(halo, halo, halo_sem.at[1]).wait()

    def product_block(b, carry):
        cols = at(b, 128)
        parts = []
        for r in range(4):
            rows = pl.ds(r * 128, 128)
            sides = []
            for j in range(3):
                if r == 0:
                    before = pltpu.roll(halo[:, cols].astype(f32), 14 - 2 * j, 0)
                    before = jnp.where(me > 0, before, jnp.zeros_like(before))
                else:
                    before = sv[j, pl.ds(r * 128 - 16, 16), cols].astype(f32)
                now = sv[j, rows, cols].astype(f32)
                wide = jnp.concatenate([before[8:], now], 0)
                sides.append(
                    taps[0, pl.ds(j, 1), cols] * now
                    + taps[1, pl.ds(j, 1), cols] * pltpu.roll(wide, 1, 0)[8:]
                    + taps[2, pl.ds(j, 1), cols] * pltpu.roll(wide, 2, 0)[8:]
                )
            product = sides[1] * sides[2]
            gate[rows, cols] = sides[0]
            extra[rows, cols] = skip[:, cols] * product
            parts.append(product.astype(bf16))
        send_x[block_at(1, b)] = dot_t(t["pick"][...], jnp.concatenate(parts, 1)).astype(bf16)
        return carry

    for q in range(0, PIECES, STEPS[1]):
        lax.fori_loop(2 * q, 2 * (q + STEPS[1]), product_block, 0, unroll=2)
        send(1, send_x, recv_x, q)

    weight_copy = pltpu.make_async_remote_copy(
        src_ref=weight_in.at[:, at(1 - tp, 2048)],
        dst_ref=wb,
        send_sem=pair_send.at[PIECES],
        recv_sem=pair_recv.at[PIECES],
        device_id=(me, 1 - tp),
        device_id_type=MESH,
    )
    weight_copy.start()

    for i, copy in enumerate(load_t):
        if NAMES[i] != "pick":
            copy.wait()

    for q in range(0, PIECES, STEPS[0]):
        arrived(0, recv_h, q, link_recv)
        for k in range(STEPS[0]):
            xs[k] = spread(t["swap"], recv_h, *place(q + k, STEPS[0]))
        for k in range(STEPS[0]):
            spec[q + k] = forward(t, xs[k])

    for q in range(0, PIECES, STEPS[1]):
        arrived(1, recv_x, q, link_recv)
        for k in range(STEPS[1]):
            xs[k] = spread(t["swap"], recv_x, *place(q + k, STEPS[1]))
        for k in range(STEPS[1]):
            sx[k] = forward(t, xs[k])
        for k in range(STEPS[1]):
            for m in range(2):
                rows = pl.ds(m * 512, 512)
                ys[k, :, pl.ds(m * 256, 256)] = backward(t, sx[k, rows, :], spec[q + k, rows, :], 2)
        for k in range(STEPS[1]):
            gather(t["swap"], ys[k], send_y, *place(q + k, STEPS[2]))
        if STEPS[2] <= STEPS[1]:
            for k in range(0, STEPS[1], STEPS[2]):
                send(2, send_y, recv_y, q + k)

    load_w.wait()
    weight_copy.wait()
    copies = []

    def gate_block(b, carry):
        conv = dot(recv_y[block_at(2, b)].astype(f32).T.astype(bf16), t["pick"][...])
        for part in range(PIECES):
            rows, cols = pl.ds(part * PART, PART), at(b, 128)
            ga[rows, cols] = (gate[rows, cols] * (conv[:, part * 128 : part * 128 + 128] + extra[rows, cols])).astype(bf16)
        return carry

    def gated(q):
        arrived(2, recv_y, q, link_recv)
        lax.fori_loop(2 * q, 2 * (q + STEPS[2]), gate_block, 0, unroll=2)
        chans = pl.ds(q * WIDTH, STEPS[2] * WIDTH)
        copy = pltpu.make_async_remote_copy(
            src_ref=ga.at[:, chans],
            dst_ref=gb.at[:, chans],
            send_sem=pair_send.at[q],
            recv_sem=pair_recv.at[q],
            device_id=(me, 1 - tp),
            device_id_type=MESH,
        )
        copy.start()
        copies.append(copy)

    early = PIECES - STEPS[2]
    for q in range(0, early, STEPS[2]):
        gated(q)
    for copy in copies:
        copy.wait()
    first, final = pl.ds(0, early * WIDTH), pl.ds(early * WIDTH, STEPS[2] * WIDTH)

    def project_first(i, carry):
        cols = at(i, 256)
        left = jnp.concatenate([ga[:, first], gb[:, first]], 1)
        acc[:, cols] = dot(left, jnp.concatenate([wa[first, cols], wb[first, cols]], 0))
        return carry

    lax.fori_loop(0, 8, project_first, 0, unroll=2)
    gated(early)

    def project_own(i, carry):
        cols = at(i, 256)
        acc[:, cols] = acc[:, cols] + dot(ga[:, final], wa[final, cols])
        return carry

    lax.fori_loop(0, 8, project_own, 0, unroll=2)
    copies[-1].wait()

    def out_copy(i):
        return pltpu.make_async_copy(done.at[:, at(i, 512)], out.at[:, at(i, 512)], out_sem.at[i])

    def finish(i, carry):
        for half in range(2):
            cols = at(2 * i + half, 256)
            done[:, cols] = (acc[:, cols] + dot(gb[:, final], wb[final, cols])).astype(bf16)
        out_copy(i).start()
        return carry

    lax.fori_loop(0, 4, finish, 0)
    for i in range(4):
        out_copy(i).wait()
    pltpu.make_async_copy(tail, tail, halo_sem.at[0]).wait()
    for array, buf in ((0, send_h), (1, send_x), (2, send_y)):
        for q in range(0, PIECES, STEPS[array]):
            arrived(array, buf, q, link_send)


def handed_on(src, dst, held, sem):
    rows = [pl.ds(i * 128, 128) for i in range(4)]
    reads = [pltpu.make_async_copy(src.at[r], held.at[r], sem.at[0, i]) for i, r in enumerate(rows)]
    writes = [pltpu.make_async_copy(held.at[r], dst.at[r], sem.at[1, i]) for i, r in enumerate(rows)]
    for copy in reads:
        copy.start()
    for i in range(4):
        reads[i].wait()
        writes[i].start()
    for copy in writes:
        copy.wait()


def body(streams, short_filter, long_filter, skip_gain, out_weight):
    consts = tables()
    consts = [jnp.asarray(consts[name]) for name in NAMES]
    hbm = pl.BlockSpec(memory_space=pl.ANY)
    vmem = pl.BlockSpec(memory_space=pltpu.VMEM)
    links = [pltpu.VMEM((PIECES // step * 1024, step * PART), bf16) for step in STEPS]
    dma = pltpu.SemaphoreType.DMA
    result = pl.pallas_call(
        kernel,
        out_shape=jax.ShapeDtypeStruct((512, 2048), bf16),
        in_specs=[hbm, hbm, hbm, vmem, vmem] + [hbm] * len(NAMES),
        out_specs=hbm,
        scratch_shapes=[pltpu.VMEM(c.shape, c.dtype) for c in consts]
        + [
            pltpu.VMEM((3, 512, 1024), bf16),
            pltpu.VMEM((512, 1024), f32),
            pltpu.VMEM((16, 1024), bf16),
            pltpu.VMEM((16, 1024), bf16),
            pltpu.VMEM((512, 1024), f32),
            pltpu.VMEM((512, 1024), f32),
            *links,
            *links,
            pltpu.VMEM((2, 256, 512), bf16),
            pltpu.VMEM((2, 1024, 256), f32),
            pltpu.VMEM((2, 256, 512), bf16),
            pltpu.VMEM((PIECES, OWN * 256, 256), f32),
            pltpu.VMEM((1024, 2048), bf16),
            pltpu.VMEM((1024, 2048), bf16),
            pltpu.VMEM((512, 1024), bf16),
            pltpu.VMEM((512, 1024), bf16),
            pltpu.VMEM((512, 2048), f32),
            pltpu.VMEM((512, 2048), bf16),
            dma((3,)),
            dma((len(NAMES),)),
            dma((3 * PIECES,)),
            dma((3 * PIECES,)),
            dma((PIECES + 1,)),
            dma((PIECES + 1,)),
            dma((2,)),
            dma((4,)),
        ],
        compiler_params=pltpu.CompilerParams(collective_id=0, has_side_effects=True, vmem_limit_bytes=60 << 20),
        name="hyena",
    )(jnp.transpose(streams, (1, 0, 2)), long_filter, out_weight, short_filter, skip_gain[None, :], *consts)
    return pl.pallas_call(
        handed_on,
        out_shape=jax.ShapeDtypeStruct((512, 2048), bf16),
        in_specs=[hbm],
        out_specs=hbm,
        scratch_shapes=[pltpu.VMEM((512, 2048), bf16), dma((2, 4))],
        name="handed_on",
    )(result)


def solution(mesh):
    return jax.shard_map(
        body,
        mesh=mesh,
        in_specs=(
            P("ctx", None, "tp"),
            P(None, None, "tp"),
            P("ctx", "tp"),
            P("tp"),
            P("tp", None),
        ),
        out_specs=P("ctx", "tp"),
        check_vma=False,
    )
```

```python
import functools
import itertools
import random

import jax
import jax.numpy as jnp
import ml_dtypes
import numpy as np
from jax import lax
from jax.experimental import pallas as pl
from jax.experimental.pallas import tpu as pltpu
from jax.sharding import PartitionSpec as P

MESH = pl.DeviceIdType.MESH
bf16, f32 = jnp.bfloat16, jnp.float32

PIECES = 4
OWN = 16 // PIECES
PART = 512 // PIECES
BLOCK = 128 * PIECES
WIDTH = 1024 // PIECES
STEPS = (2, 1, 1)


def split(a):
    high = a.astype(ml_dtypes.bfloat16)
    return high, (a - high.astype(np.float64)).astype(ml_dtypes.bfloat16)


def tables():
    k1 = np.arange(256) + 0.5
    row = np.arange(256)
    angle = 2 * np.pi * np.outer(k1, 4 * (row % 64) + row // 64) / 512
    first = np.concatenate(split(np.concatenate([np.cos(angle), -np.sin(angle)], 0)), 0)
    twist = 2 * np.pi * np.outer(k1, np.arange(128)) / 65536
    inner = 2 * np.pi * (np.outer(np.arange(128), np.arange(128)) % 128) / 128
    c, s = np.cos(inner), np.sin(inner)
    sh, sl = split(np.block([[c, -s], [s, c]]))
    bh, bl = split(np.block([[c, s], [-s, c]]))
    last = np.concatenate(split(np.concatenate([np.cos(angle.T), -np.sin(angle.T)], 1) * (2.0 / 65536)), 0)
    r = np.arange(256)
    swap = np.zeros((256, 256), ml_dtypes.bfloat16)
    swap[r, (r % 16) * 16 + r // 16] = 1
    r = np.arange(BLOCK)
    pick = np.zeros((BLOCK, BLOCK), ml_dtypes.bfloat16)
    pick[r, (r % PIECES) * 128 + r // PIECES] = 1
    return dict(
        first=first,
        tcos=np.cos(twist).astype(np.float32),
        tsin=np.sin(twist).astype(np.float32),
        second=np.concatenate([sh, sh, sl], 0),
        back=np.concatenate([bh, bh, bl], 0),
        last=last,
        swap=swap,
        pick=pick,
    )


def offsets():
    every = [d for d in itertools.product(range(4), repeat=3) if d != (0, 0, 0)]
    random.Random(1).shuffle(every)
    order = []
    for d in sorted(every, key=lambda d: -sum(min(v, 4 - v) for v in d)):
        for e in (d, (d[1], d[2], d[0]), (d[2], d[0], d[1])):
            for g in (e, tuple(-v % 4 for v in e)):
                if g not in order:
                    order.append(g)
    return order


def dot(a, b):
    return jnp.dot(a, b, preferred_element_type=f32)


def dot_t(a, b):
    return lax.dot_general(a, b, (((1,), (1,)), ((), ())), preferred_element_type=f32)


def halves(v):
    high = v.astype(bf16)
    return high, (v - high.astype(f32)).astype(bf16)


def at(i, size):
    return pl.ds(pl.multiple_of(i * size, size), size)


def stack(tiles, rows, columns):
    return jnp.concatenate([jnp.concatenate([tiles(r, c) for r in range(rows)], 0) for c in range(columns)], 1)


def place(q, step):
    return (q // step) * 1024, (q % step) * 128


def spread(swap, src, row, lane):
    rows = jnp.concatenate(
        [src[pl.ds(pl.multiple_of(row + g * 256, 256), 256), pl.ds(lane, 128)] for g in range(4)], 1
    )
    mixed = dot(swap[...], rows).astype(bf16)

    def tile(r, c):
        part, g = r // 4, r % 4
        low = (c * PIECES + part) * 16
        return mixed[low : low + 16, g * 128 : g * 128 + 128]

    return stack(tile, 16, OWN)


def gather(swap, y, dst, row, lane):
    def tile(r, g):
        c, part = r // PIECES, r % PIECES
        low = part * 64 + g * 16
        return y[low : low + 16, c * 128 : c * 128 + 128]

    mixed = dot(swap[...], stack(tile, 16, 4)).astype(bf16)
    for g in range(4):
        dst[pl.ds(pl.multiple_of(row + g * 256, 256), 256), pl.ds(lane, 128)] = mixed[:, g * 128 : g * 128 + 128]


def forward(t, x):
    a = dot(t["first"][...], x)
    re = a[0:256] + a[512:768]
    im = a[256:512] + a[768:1024]
    tc, ts = t["tcos"][...], t["tsin"][...]
    parts = []
    for c in range(OWN):
        r, i = re[:, c * 128 : c * 128 + 128], im[:, c * 128 : c * 128 + 128]
        parts.append(jnp.concatenate([r * tc + i * ts, i * tc - r * ts], 1))
    zh, zl = halves(jnp.concatenate(parts, 0))
    return dot(jnp.concatenate([zh, zl, zh], 1), t["second"][...])


def backward(t, sx, sh, count):
    xr, xi, hr, hi = sx[:, :128], sx[:, 128:], sh[:, :128], sh[:, 128:]
    yh, yl = halves(jnp.concatenate([xr * hr - xi * hi, xr * hi + xi * hr], 1))
    b = dot(jnp.concatenate([yh, yl, yh], 1), t["back"][...])
    tc, ts = t["tcos"][...], t["tsin"][...]
    res, ims = [], []
    for c in range(count):
        r, i = b[c * 256 : c * 256 + 256, :128], b[c * 256 : c * 256 + 256, 128:]
        res.append(r * tc - i * ts)
        ims.append(i * tc + r * ts)
    vh, vl = halves(jnp.concatenate([jnp.concatenate(res, 1), jnp.concatenate(ims, 1)], 0))
    o = dot(t["last"][...], vh)
    return (o[:256] + o[256:] + dot(t["last"][:256, :], vl)).astype(bf16)


NAMES = ("first", "tcos", "tsin", "second", "back", "last", "swap", "pick")


def kernel(*refs):
    n = len(NAMES)
    streams_in, filter_in, weight_in = refs[:3]
    taps, skip = refs[3:5]
    table_in = refs[5 : 5 + n]
    out = refs[5 + n]
    tabs = refs[6 + n : 6 + 2 * n]
    (sv, hv, tail, halo, gate, extra, send_h, send_x, send_y, recv_h, recv_x, recv_y) = refs[6 + 2 * n : 18 + 2 * n]
    (xs, sx, ys, spec, wa, wb, ga, gb, acc, done) = refs[18 + 2 * n : 28 + 2 * n]
    load_sem, table_sem, link_send, link_recv, pair_send, pair_recv, halo_sem, out_sem = refs[28 + 2 * n :]
    t = dict(zip(NAMES, tabs))

    me, tp = lax.axis_index("ctx"), lax.axis_index("tp")
    mz, mx, my = me // 16, lax.rem(me // 4, 4), lax.rem(me, 4)
    along = [[lax.rem(m + i, 4) * scale for i in range(4)] for m, scale in ((mz, 16), (mx, 4), (my, 1))]
    order = offsets()

    def peer(d):
        return along[0][d[0]] + along[1][d[1]] + along[2][d[2]]

    load_h = pltpu.make_async_copy(filter_in, hv, load_sem.at[0])
    load_s = pltpu.make_async_copy(streams_in, sv, load_sem.at[1])
    load_w = pltpu.make_async_copy(weight_in.at[:, at(tp, 2048)], wa, load_sem.at[2])
    load_t = [pltpu.make_async_copy(a, b, table_sem.at[i]) for i, (a, b) in enumerate(zip(table_in, tabs))]
    load_t[NAMES.index("pick")].start()
    for i in range(4):
        part = pl.ds(i * 128, 128)
        pltpu.make_async_copy(filter_in.at[part], hv.at[part], load_sem.at[0]).start()
    for i in range(6):
        part = (i // 2, pl.ds(i % 2 * 256, 256))
        pltpu.make_async_copy(streams_in.at[part], sv.at[part], load_sem.at[1]).start()

    barrier = pltpu.get_barrier_semaphore()
    for d in order:
        pl.semaphore_signal(barrier, inc=1, device_id=(peer(d), tp), device_id_type=MESH)
    pl.semaphore_signal(barrier, inc=1, device_id=(me, 1 - tp), device_id_type=MESH)


    def send(array, src, dst, q):
        base = (q // STEPS[array]) * 1024
        for d in order:
            p = peer(d)
            pltpu.make_async_remote_copy(
                src_ref=src.at[pl.ds(pl.multiple_of(base + p * 16, 16), 16)],
                dst_ref=dst.at[pl.ds(pl.multiple_of(base + me * 16, 16), 16)],
                send_sem=link_send.at[array * PIECES + q],
                recv_sem=link_recv.at[array * PIECES + q],
                device_id=(p, tp),
                device_id_type=MESH,
            ).start()
        mine = pl.ds(pl.multiple_of(base + me * 16, 16), 16)
        dst[mine, :] = src[mine, :]

    def arrived(array, buf, q, sem):
        view = buf.at[pl.ds(0, 63 * 16)]
        pltpu.make_async_copy(view, view, sem.at[array * PIECES + q]).wait()

    def block_at(array, b):
        row, lane = place(b // 2, STEPS[array])
        return pl.ds(pl.multiple_of(row + (b % 2) * BLOCK, BLOCK), BLOCK), pl.ds(pl.multiple_of(lane, 128), 128)

    load_t[NAMES.index("pick")].wait()
    load_h.wait()

    def filter_block(b, carry):
        parts = [hv[pl.ds(part * PART, PART), at(b, 128)].astype(bf16) for part in range(PIECES)]
        send_h[block_at(0, b)] = dot_t(t["pick"][...], jnp.concatenate(parts, 1)).astype(bf16)
        return carry

    lax.fori_loop(0, 8, filter_block, 0, unroll=4)

    load_s.wait()
    for i, copy in enumerate(load_t):
        if NAMES[i] != "pick":
            copy.start()
    load_w.start()
    line = lax.broadcasted_iota(jnp.int32, (16, 1024), 0)
    packed = jnp.zeros((16, 1024), f32)
    for j in range(3):
        rows = pltpu.roll(sv[j, pl.ds(496, 16), :].astype(f32), 2 + 2 * j, 0)
        packed = jnp.where((line >= 2 * j) & (line < 2 * j + 2), rows, packed)
    tail[...] = packed.astype(bf16)

    pl.semaphore_wait(barrier, 64)
    after = lax.rem(me + 1, 64)
    for i in range(4):
        pltpu.make_async_remote_copy(
            src_ref=tail.at[:, pl.ds(i * 256, 256)],
            dst_ref=halo.at[:, pl.ds(i * 256, 256)],
            send_sem=halo_sem.at[0],
            recv_sem=halo_sem.at[1],
            device_id=(after, tp),
            device_id_type=MESH,
        ).start()
    for q in range(0, PIECES, STEPS[0]):
        send(0, send_h, recv_h, q)
    pltpu.make_async_copy(halo, halo, halo_sem.at[1]).wait()

    def product_block(b, carry):
        cols = at(b, 128)
        parts = []
        for r in range(4):
            rows = pl.ds(r * 128, 128)
            sides = []
            for j in range(3):
                if r == 0:
                    before = pltpu.roll(halo[:, cols].astype(f32), 14 - 2 * j, 0)
                    before = jnp.where(me > 0, before, jnp.zeros_like(before))
                else:
                    before = sv[j, pl.ds(r * 128 - 16, 16), cols].astype(f32)
                now = sv[j, rows, cols].astype(f32)
                wide = jnp.concatenate([before[8:], now], 0)
                sides.append(
                    taps[0, pl.ds(j, 1), cols] * now
                    + taps[1, pl.ds(j, 1), cols] * pltpu.roll(wide, 1, 0)[8:]
                    + taps[2, pl.ds(j, 1), cols] * pltpu.roll(wide, 2, 0)[8:]
                )
            product = sides[1] * sides[2]
            gate[rows, cols] = sides[0]
            extra[rows, cols] = skip[:, cols] * product
            parts.append(product.astype(bf16))
        send_x[block_at(1, b)] = dot_t(t["pick"][...], jnp.concatenate(parts, 1)).astype(bf16)
        return carry

    for q in range(0, PIECES, STEPS[1]):
        lax.fori_loop(2 * q, 2 * (q + STEPS[1]), product_block, 0, unroll=2)
        send(1, send_x, recv_x, q)

    weight_copy = pltpu.make_async_remote_copy(
        src_ref=weight_in.at[:, at(1 - tp, 2048)],
        dst_ref=wb,
        send_sem=pair_send.at[PIECES],
        recv_sem=pair_recv.at[PIECES],
        device_id=(me, 1 - tp),
        device_id_type=MESH,
    )
    weight_copy.start()

    for i, copy in enumerate(load_t):
        if NAMES[i] != "pick":
            copy.wait()

    for q in range(0, PIECES, STEPS[0]):
        arrived(0, recv_h, q, link_recv)
        for k in range(STEPS[0]):
            xs[k] = spread(t["swap"], recv_h, *place(q + k, STEPS[0]))
        for k in range(STEPS[0]):
            spec[q + k] = forward(t, xs[k])

    for q in range(0, PIECES, STEPS[1]):
        arrived(1, recv_x, q, link_recv)
        for k in range(STEPS[1]):
            xs[k] = spread(t["swap"], recv_x, *place(q + k, STEPS[1]))
        for k in range(STEPS[1]):
            sx[k] = forward(t, xs[k])
        for k in range(STEPS[1]):
            for m in range(2):
                rows = pl.ds(m * 512, 512)
                ys[k, :, pl.ds(m * 256, 256)] = backward(t, sx[k, rows, :], spec[q + k, rows, :], 2)
        for k in range(STEPS[1]):
            gather(t["swap"], ys[k], send_y, *place(q + k, STEPS[2]))
        if STEPS[2] <= STEPS[1]:
            for k in range(0, STEPS[1], STEPS[2]):
                send(2, send_y, recv_y, q + k)

    load_w.wait()
    weight_copy.wait()
    copies = []

    def gate_block(b, carry):
        conv = dot(recv_y[block_at(2, b)].astype(f32).T.astype(bf16), t["pick"][...])
        for part in range(PIECES):
            rows, cols = pl.ds(part * PART, PART), at(b, 128)
            ga[rows, cols] = (gate[rows, cols] * (conv[:, part * 128 : part * 128 + 128] + extra[rows, cols])).astype(bf16)
        return carry

    def gated(q):
        arrived(2, recv_y, q, link_recv)
        lax.fori_loop(2 * q, 2 * (q + STEPS[2]), gate_block, 0, unroll=2)
        chans = pl.ds(q * WIDTH, STEPS[2] * WIDTH)
        copy = pltpu.make_async_remote_copy(
            src_ref=ga.at[:, chans],
            dst_ref=gb.at[:, chans],
            send_sem=pair_send.at[q],
            recv_sem=pair_recv.at[q],
            device_id=(me, 1 - tp),
            device_id_type=MESH,
        )
        copy.start()
        copies.append(copy)

    early = PIECES - STEPS[2]
    for q in range(0, early, STEPS[2]):
        gated(q)
    for copy in copies:
        copy.wait()
    first, final = pl.ds(0, early * WIDTH), pl.ds(early * WIDTH, STEPS[2] * WIDTH)

    def project_first(i, carry):
        cols = at(i, 256)
        left = jnp.concatenate([ga[:, first], gb[:, first]], 1)
        acc[:, cols] = dot(left, jnp.concatenate([wa[first, cols], wb[first, cols]], 0))
        return carry

    lax.fori_loop(0, 8, project_first, 0, unroll=2)
    gated(early)

    def project_own(i, carry):
        cols = at(i, 256)
        acc[:, cols] = acc[:, cols] + dot(ga[:, final], wa[final, cols])
        return carry

    lax.fori_loop(0, 8, project_own, 0, unroll=2)
    copies[-1].wait()

    def out_copy(i):
        return pltpu.make_async_copy(done.at[:, at(i, 512)], out.at[:, at(i, 512)], out_sem.at[i])

    def finish(i, carry):
        for half in range(2):
            cols = at(2 * i + half, 256)
            done[:, cols] = (acc[:, cols] + dot(gb[:, final], wb[final, cols])).astype(bf16)
        out_copy(i).start()
        return carry

    lax.fori_loop(0, 4, finish, 0)
    for i in range(4):
        out_copy(i).wait()
    pltpu.make_async_copy(tail, tail, halo_sem.at[0]).wait()
    for array, buf in ((0, send_h), (1, send_x), (2, send_y)):
        for q in range(0, PIECES, STEPS[array]):
            arrived(array, buf, q, link_send)


def handed_on(src, dst, held, sem):
    rows = [pl.ds(i * 128, 128) for i in range(4)]
    reads = [pltpu.make_async_copy(src.at[r], held.at[r], sem.at[0, i]) for i, r in enumerate(rows)]
    writes = [pltpu.make_async_copy(held.at[r], dst.at[r], sem.at[1, i]) for i, r in enumerate(rows)]
    for copy in reads:
        copy.start()
    for read, write in zip(reads, writes):
        read.wait()
        write.start()
    for copy in writes:
        copy.wait()


def body(streams, short_filter, long_filter, skip_gain, out_weight):
    consts = tables()
    consts = [jnp.asarray(consts[name]) for name in NAMES]
    hbm = pl.BlockSpec(memory_space=pl.ANY)
    vmem = pl.BlockSpec(memory_space=pltpu.VMEM)
    links = [pltpu.VMEM((PIECES // step * 1024, step * PART), bf16) for step in STEPS]
    dma = pltpu.SemaphoreType.DMA
    result = pl.pallas_call(
        kernel,
        out_shape=jax.ShapeDtypeStruct((512, 2048), bf16),
        in_specs=[hbm, hbm, hbm, vmem, vmem] + [hbm] * len(NAMES),
        out_specs=hbm,
        scratch_shapes=[pltpu.VMEM(c.shape, c.dtype) for c in consts]
        + [
            pltpu.VMEM((3, 512, 1024), bf16),
            pltpu.VMEM((512, 1024), f32),
            pltpu.VMEM((16, 1024), bf16),
            pltpu.VMEM((16, 1024), bf16),
            pltpu.VMEM((512, 1024), f32),
            pltpu.VMEM((512, 1024), f32),
            *links,
            *links,
            pltpu.VMEM((2, 256, 512), bf16),
            pltpu.VMEM((2, 1024, 256), f32),
            pltpu.VMEM((2, 256, 512), bf16),
            pltpu.VMEM((PIECES, OWN * 256, 256), f32),
            pltpu.VMEM((1024, 2048), bf16),
            pltpu.VMEM((1024, 2048), bf16),
            pltpu.VMEM((512, 1024), bf16),
            pltpu.VMEM((512, 1024), bf16),
            pltpu.VMEM((512, 2048), f32),
            pltpu.VMEM((512, 2048), bf16),
            dma((3,)),
            dma((len(NAMES),)),
            dma((3 * PIECES,)),
            dma((3 * PIECES,)),
            dma((PIECES + 1,)),
            dma((PIECES + 1,)),
            dma((2,)),
            dma((4,)),
        ],
        compiler_params=pltpu.CompilerParams(collective_id=0, has_side_effects=True, vmem_limit_bytes=60 << 20),
        name="hyena",
    )(jnp.transpose(streams, (1, 0, 2)), long_filter, out_weight, short_filter, skip_gain[None, :], *consts)
    return pl.pallas_call(
        handed_on,
        out_shape=jax.ShapeDtypeStruct((512, 2048), bf16),
        in_specs=[hbm],
        out_specs=hbm,
        scratch_shapes=[pltpu.VMEM((512, 2048), bf16), dma((2, 4))],
        name="handed_on",
    )(result)


def solution(mesh):
    return jax.shard_map(
        body,
        mesh=mesh,
        in_specs=(
            P("ctx", None, "tp"),
            P(None, None, "tp"),
            P("ctx", "tp"),
            P("tp"),
            P("tp", None),
        ),
        out_specs=P("ctx", "tp"),
        check_vma=False,
    )
```

```python
import functools
import itertools
import random

import jax
import jax.numpy as jnp
import ml_dtypes
import numpy as np
from jax import lax
from jax.experimental import pallas as pl
from jax.experimental.pallas import tpu as pltpu
from jax.sharding import PartitionSpec as P

MESH = pl.DeviceIdType.MESH
bf16, f32 = jnp.bfloat16, jnp.float32

PIECES = 4
OWN = 16 // PIECES
PART = 512 // PIECES
BLOCK = 128 * PIECES
WIDTH = 1024 // PIECES
STEPS = (2, 1, 1)


def split(a):
    high = a.astype(ml_dtypes.bfloat16)
    return high, (a - high.astype(np.float64)).astype(ml_dtypes.bfloat16)


def tables():
    k1 = np.arange(256) + 0.5
    row = np.arange(256)
    angle = 2 * np.pi * np.outer(k1, 4 * (row % 64) + row // 64) / 512
    first = np.concatenate(split(np.concatenate([np.cos(angle), -np.sin(angle)], 0)), 0)
    twist = 2 * np.pi * np.outer(k1, np.arange(128)) / 65536
    inner = 2 * np.pi * (np.outer(np.arange(128), np.arange(128)) % 128) / 128
    c, s = np.cos(inner), np.sin(inner)
    sh, sl = split(np.block([[c, -s], [s, c]]))
    bh, bl = split(np.block([[c, s], [-s, c]]))
    last = np.concatenate(split(np.concatenate([np.cos(angle.T), -np.sin(angle.T)], 1) * (2.0 / 65536)), 0)
    r = np.arange(256)
    swap = np.zeros((256, 256), ml_dtypes.bfloat16)
    swap[r, (r % 16) * 16 + r // 16] = 1
    r = np.arange(BLOCK)
    pick = np.zeros((BLOCK, BLOCK), ml_dtypes.bfloat16)
    pick[r, (r % PIECES) * 128 + r // PIECES] = 1
    return dict(
        first=first,
        tcos=np.cos(twist).astype(np.float32),
        tsin=np.sin(twist).astype(np.float32),
        second=np.concatenate([sh, sh, sl], 0),
        back=np.concatenate([bh, bh, bl], 0),
        last=last,
        swap=swap,
        pick=pick,
    )


def offsets():
    every = [d for d in itertools.product(range(4), repeat=3) if d != (0, 0, 0)]
    random.Random(1).shuffle(every)
    order = []
    for d in sorted(every, key=lambda d: -sum(min(v, 4 - v) for v in d)):
        for e in (d, (d[1], d[2], d[0]), (d[2], d[0], d[1])):
            for g in (e, tuple(-v % 4 for v in e)):
                if g not in order:
                    order.append(g)
    return order


def dot(a, b):
    return jnp.dot(a, b, preferred_element_type=f32)


def dot_t(a, b):
    return lax.dot_general(a, b, (((1,), (1,)), ((), ())), preferred_element_type=f32)


def halves(v):
    high = v.astype(bf16)
    return high, (v - high.astype(f32)).astype(bf16)


def at(i, size):
    return pl.ds(pl.multiple_of(i * size, size), size)


def stack(tiles, rows, columns):
    return jnp.concatenate([jnp.concatenate([tiles(r, c) for r in range(rows)], 0) for c in range(columns)], 1)


def place(q, step):
    return (q // step) * 1024, (q % step) * 128


def spread(swap, src, row, lane):
    rows = jnp.concatenate(
        [src[pl.ds(pl.multiple_of(row + g * 256, 256), 256), pl.ds(lane, 128)] for g in range(4)], 1
    )
    mixed = dot(swap[...], rows).astype(bf16)

    def tile(r, c):
        part, g = r // 4, r % 4
        low = (c * PIECES + part) * 16
        return mixed[low : low + 16, g * 128 : g * 128 + 128]

    return stack(tile, 16, OWN)


def gather(swap, y, dst, row, lane):
    def tile(r, g):
        c, part = r // PIECES, r % PIECES
        low = part * 64 + g * 16
        return y[low : low + 16, c * 128 : c * 128 + 128]

    mixed = dot(swap[...], stack(tile, 16, 4)).astype(bf16)
    for g in range(4):
        dst[pl.ds(pl.multiple_of(row + g * 256, 256), 256), pl.ds(lane, 128)] = mixed[:, g * 128 : g * 128 + 128]


def forward(t, x):
    a = dot(t["first"][...], x)
    re = a[0:256] + a[512:768]
    im = a[256:512] + a[768:1024]
    tc, ts = t["tcos"][...], t["tsin"][...]
    parts = []
    for c in range(OWN):
        r, i = re[:, c * 128 : c * 128 + 128], im[:, c * 128 : c * 128 + 128]
        parts.append(jnp.concatenate([r * tc + i * ts, i * tc - r * ts], 1))
    zh, zl = halves(jnp.concatenate(parts, 0))
    return dot(jnp.concatenate([zh, zl, zh], 1), t["second"][...])


def backward(t, sx, sh, count):
    xr, xi, hr, hi = sx[:, :128], sx[:, 128:], sh[:, :128], sh[:, 128:]
    yh, yl = halves(jnp.concatenate([xr * hr - xi * hi, xr * hi + xi * hr], 1))
    b = dot(jnp.concatenate([yh, yl, yh], 1), t["back"][...])
    tc, ts = t["tcos"][...], t["tsin"][...]
    res, ims = [], []
    for c in range(count):
        r, i = b[c * 256 : c * 256 + 256, :128], b[c * 256 : c * 256 + 256, 128:]
        res.append(r * tc - i * ts)
        ims.append(i * tc + r * ts)
    vh, vl = halves(jnp.concatenate([jnp.concatenate(res, 1), jnp.concatenate(ims, 1)], 0))
    o = dot(t["last"][...], vh)
    return (o[:256] + o[256:] + dot(t["last"][:256, :], vl)).astype(bf16)


NAMES = ("first", "tcos", "tsin", "second", "back", "last", "swap", "pick")


def kernel(*refs):
    n = len(NAMES)
    streams_in, filter_in, weight_in = refs[:3]
    taps, skip = refs[3:5]
    table_in = refs[5 : 5 + n]
    out = refs[5 + n]
    tabs = refs[6 + n : 6 + 2 * n]
    (sv, hv, tail, halo, gate, extra, send_h, send_x, send_y, recv_h, recv_x, recv_y) = refs[6 + 2 * n : 18 + 2 * n]
    (xs, sx, ys, spec, wa, wb, ga, gb, acc, done) = refs[18 + 2 * n : 28 + 2 * n]
    load_sem, table_sem, link_send, link_recv, pair_send, pair_recv, halo_sem, out_sem = refs[28 + 2 * n :]
    t = dict(zip(NAMES, tabs))

    me, tp = lax.axis_index("ctx"), lax.axis_index("tp")
    mz, mx, my = me // 16, lax.rem(me // 4, 4), lax.rem(me, 4)
    along = [[lax.rem(m + i, 4) * scale for i in range(4)] for m, scale in ((mz, 16), (mx, 4), (my, 1))]
    order = offsets()

    def peer(d):
        return along[0][d[0]] + along[1][d[1]] + along[2][d[2]]

    load_h = pltpu.make_async_copy(filter_in, hv, load_sem.at[0])
    load_s = pltpu.make_async_copy(streams_in, sv, load_sem.at[1])
    load_w = pltpu.make_async_copy(weight_in.at[:, at(tp, 2048)], wa, load_sem.at[2])
    load_t = [pltpu.make_async_copy(a, b, table_sem.at[i]) for i, (a, b) in enumerate(zip(table_in, tabs))]
    load_t[NAMES.index("pick")].start()
    for i in range(4):
        part = pl.ds(i * 128, 128)
        pltpu.make_async_copy(filter_in.at[part], hv.at[part], load_sem.at[0]).start()
    for i in range(6):
        part = (i // 2, pl.ds(i % 2 * 256, 256))
        pltpu.make_async_copy(streams_in.at[part], sv.at[part], load_sem.at[1]).start()

    barrier = pltpu.get_barrier_semaphore()
    for d in order:
        pl.semaphore_signal(barrier, inc=1, device_id=(peer(d), tp), device_id_type=MESH)
    pl.semaphore_signal(barrier, inc=1, device_id=(me, 1 - tp), device_id_type=MESH)


    def send(array, src, dst, q):
        base = (q // STEPS[array]) * 1024
        for d in order:
            p = peer(d)
            pltpu.make_async_remote_copy(
                src_ref=src.at[pl.ds(pl.multiple_of(base + p * 16, 16), 16)],
                dst_ref=dst.at[pl.ds(pl.multiple_of(base + me * 16, 16), 16)],
                send_sem=link_send.at[array * PIECES + q],
                recv_sem=link_recv.at[array * PIECES + q],
                device_id=(p, tp),
                device_id_type=MESH,
            ).start()
        mine = pl.ds(pl.multiple_of(base + me * 16, 16), 16)
        dst[mine, :] = src[mine, :]

    def arrived(array, buf, q, sem):
        view = buf.at[pl.ds(0, 63 * 16)]
        pltpu.make_async_copy(view, view, sem.at[array * PIECES + q]).wait()

    def block_at(array, b):
        row, lane = place(b // 2, STEPS[array])
        return pl.ds(pl.multiple_of(row + (b % 2) * BLOCK, BLOCK), BLOCK), pl.ds(pl.multiple_of(lane, 128), 128)

    load_t[NAMES.index("pick")].wait()
    load_h.wait()

    def filter_block(b, carry):
        parts = [hv[pl.ds(part * PART, PART), at(b, 128)].astype(bf16) for part in range(PIECES)]
        send_h[block_at(0, b)] = dot_t(t["pick"][...], jnp.concatenate(parts, 1)).astype(bf16)
        return carry

    lax.fori_loop(0, 8, filter_block, 0, unroll=4)

    load_s.wait()
    for i, copy in enumerate(load_t):
        if NAMES[i] != "pick":
            copy.start()
    load_w.start()
    line = lax.broadcasted_iota(jnp.int32, (16, 1024), 0)
    packed = jnp.zeros((16, 1024), f32)
    for j in range(3):
        rows = pltpu.roll(sv[j, pl.ds(496, 16), :].astype(f32), 2 + 2 * j, 0)
        packed = jnp.where((line >= 2 * j) & (line < 2 * j + 2), rows, packed)
    tail[...] = packed.astype(bf16)

    pl.semaphore_wait(barrier, 64)
    after = lax.rem(me + 1, 64)
    for i in range(4):
        pltpu.make_async_remote_copy(
            src_ref=tail.at[:, pl.ds(i * 256, 256)],
            dst_ref=halo.at[:, pl.ds(i * 256, 256)],
            send_sem=halo_sem.at[0],
            recv_sem=halo_sem.at[1],
            device_id=(after, tp),
            device_id_type=MESH,
        ).start()
    for q in range(0, PIECES, STEPS[0]):
        send(0, send_h, recv_h, q)
    pltpu.make_async_copy(halo, halo, halo_sem.at[1]).wait()

    def product_block(b, carry):
        cols = at(b, 128)
        parts = []
        for r in range(4):
            rows = pl.ds(r * 128, 128)
            sides = []
            for j in range(3):
                if r == 0:
                    before = pltpu.roll(halo[:, cols].astype(f32), 14 - 2 * j, 0)
                    before = jnp.where(me > 0, before, jnp.zeros_like(before))
                else:
                    before = sv[j, pl.ds(r * 128 - 16, 16), cols].astype(f32)
                now = sv[j, rows, cols].astype(f32)
                wide = jnp.concatenate([before[8:], now], 0)
                sides.append(
                    taps[0, pl.ds(j, 1), cols] * now
                    + taps[1, pl.ds(j, 1), cols] * pltpu.roll(wide, 1, 0)[8:]
                    + taps[2, pl.ds(j, 1), cols] * pltpu.roll(wide, 2, 0)[8:]
                )
            product = sides[1] * sides[2]
            gate[rows, cols] = sides[0]
            extra[rows, cols] = skip[:, cols] * product
            parts.append(product.astype(bf16))
        send_x[block_at(1, b)] = dot_t(t["pick"][...], jnp.concatenate(parts, 1)).astype(bf16)
        return carry

    for q in range(0, PIECES, STEPS[1]):
        lax.fori_loop(2 * q, 2 * (q + STEPS[1]), product_block, 0, unroll=2)
        send(1, send_x, recv_x, q)

    weight_copy = pltpu.make_async_remote_copy(
        src_ref=weight_in.at[:, at(1 - tp, 2048)],
        dst_ref=wb,
        send_sem=pair_send.at[PIECES],
        recv_sem=pair_recv.at[PIECES],
        device_id=(me, 1 - tp),
        device_id_type=MESH,
    )
    weight_copy.start()

    for i, copy in enumerate(load_t):
        if NAMES[i] != "pick":
            copy.wait()

    for q in range(0, PIECES, STEPS[0]):
        arrived(0, recv_h, q, link_recv)
        for k in range(STEPS[0]):
            xs[k] = spread(t["swap"], recv_h, *place(q + k, STEPS[0]))
        for k in range(STEPS[0]):
            spec[q + k] = forward(t, xs[k])

    for q in range(0, PIECES, STEPS[1]):
        arrived(1, recv_x, q, link_recv)
        for k in range(STEPS[1]):
            xs[k] = spread(t["swap"], recv_x, *place(q + k, STEPS[1]))
        for k in range(STEPS[1]):
            sx[k] = forward(t, xs[k])
        for k in range(STEPS[1]):
            for m in range(2):
                rows = pl.ds(m * 512, 512)
                ys[k, :, pl.ds(m * 256, 256)] = backward(t, sx[k, rows, :], spec[q + k, rows, :], 2)
        for k in range(STEPS[1]):
            gather(t["swap"], ys[k], send_y, *place(q + k, STEPS[2]))
        if STEPS[2] <= STEPS[1]:
            for k in range(0, STEPS[1], STEPS[2]):
                send(2, send_y, recv_y, q + k)

    load_w.wait()
    weight_copy.wait()
    copies = []

    def gate_block(b, carry):
        conv = dot(recv_y[block_at(2, b)].astype(f32).T.astype(bf16), t["pick"][...])
        for part in range(PIECES):
            rows, cols = pl.ds(part * PART, PART), at(b, 128)
            ga[rows, cols] = (gate[rows, cols] * (conv[:, part * 128 : part * 128 + 128] + extra[rows, cols])).astype(bf16)
        return carry

    def gated(q):
        arrived(2, recv_y, q, link_recv)
        lax.fori_loop(2 * q, 2 * (q + STEPS[2]), gate_block, 0, unroll=2)
        chans = pl.ds(q * WIDTH, STEPS[2] * WIDTH)
        copy = pltpu.make_async_remote_copy(
            src_ref=ga.at[:, chans],
            dst_ref=gb.at[:, chans],
            send_sem=pair_send.at[q],
            recv_sem=pair_recv.at[q],
            device_id=(me, 1 - tp),
            device_id_type=MESH,
        )
        copy.start()
        copies.append(copy)

    early = PIECES - STEPS[2]
    for q in range(0, early, STEPS[2]):
        gated(q)
    for copy in copies:
        copy.wait()
    first, final = pl.ds(0, early * WIDTH), pl.ds(early * WIDTH, STEPS[2] * WIDTH)

    def project_first(i, carry):
        cols = at(i, 256)
        left = jnp.concatenate([ga[:, first], gb[:, first]], 1)
        acc[:, cols] = dot(left, jnp.concatenate([wa[first, cols], wb[first, cols]], 0))
        return carry

    lax.fori_loop(0, 8, project_first, 0, unroll=4)
    gated(early)

    def project_own(i, carry):
        cols = at(i, 256)
        acc[:, cols] = acc[:, cols] + dot(ga[:, final], wa[final, cols])
        return carry

    lax.fori_loop(0, 8, project_own, 0, unroll=4)
    copies[-1].wait()

    def out_copy(i):
        return pltpu.make_async_copy(done.at[:, at(i, 512)], out.at[:, at(i, 512)], out_sem.at[i])

    def finish(i, carry):
        for half in range(2):
            cols = at(2 * i + half, 256)
            done[:, cols] = (acc[:, cols] + dot(gb[:, final], wb[final, cols])).astype(bf16)
        out_copy(i).start()
        return carry

    lax.fori_loop(0, 4, finish, 0, unroll=2)
    for i in range(4):
        out_copy(i).wait()
    pltpu.make_async_copy(tail, tail, halo_sem.at[0]).wait()
    for array, buf in ((0, send_h), (1, send_x), (2, send_y)):
        for q in range(0, PIECES, STEPS[array]):
            arrived(array, buf, q, link_send)


def handed_on(src, dst, held, sem):
    rows = [pl.ds(i * 128, 128) for i in range(4)]
    reads = [pltpu.make_async_copy(src.at[r], held.at[r], sem.at[0, i]) for i, r in enumerate(rows)]
    writes = [pltpu.make_async_copy(held.at[r], dst.at[r], sem.at[1, i]) for i, r in enumerate(rows)]
    for copy in reads:
        copy.start()
    for read, write in zip(reads, writes):
        read.wait()
        write.start()
    for copy in writes:
        copy.wait()


def body(streams, short_filter, long_filter, skip_gain, out_weight):
    consts = tables()
    consts = [jnp.asarray(consts[name]) for name in NAMES]
    hbm = pl.BlockSpec(memory_space=pl.ANY)
    vmem = pl.BlockSpec(memory_space=pltpu.VMEM)
    links = [pltpu.VMEM((PIECES // step * 1024, step * PART), bf16) for step in STEPS]
    dma = pltpu.SemaphoreType.DMA
    result = pl.pallas_call(
        kernel,
        out_shape=jax.ShapeDtypeStruct((512, 2048), bf16),
        in_specs=[hbm, hbm, hbm, vmem, vmem] + [hbm] * len(NAMES),
        out_specs=hbm,
        scratch_shapes=[pltpu.VMEM(c.shape, c.dtype) for c in consts]
        + [
            pltpu.VMEM((3, 512, 1024), bf16),
            pltpu.VMEM((512, 1024), f32),
            pltpu.VMEM((16, 1024), bf16),
            pltpu.VMEM((16, 1024), bf16),
            pltpu.VMEM((512, 1024), f32),
            pltpu.VMEM((512, 1024), f32),
            *links,
            *links,
            pltpu.VMEM((2, 256, 512), bf16),
            pltpu.VMEM((2, 1024, 256), f32),
            pltpu.VMEM((2, 256, 512), bf16),
            pltpu.VMEM((PIECES, OWN * 256, 256), f32),
            pltpu.VMEM((1024, 2048), bf16),
            pltpu.VMEM((1024, 2048), bf16),
            pltpu.VMEM((512, 1024), bf16),
            pltpu.VMEM((512, 1024), bf16),
            pltpu.VMEM((512, 2048), f32),
            pltpu.VMEM((512, 2048), bf16),
            dma((3,)),
            dma((len(NAMES),)),
            dma((3 * PIECES,)),
            dma((3 * PIECES,)),
            dma((PIECES + 1,)),
            dma((PIECES + 1,)),
            dma((2,)),
            dma((4,)),
        ],
        compiler_params=pltpu.CompilerParams(collective_id=0, has_side_effects=True, vmem_limit_bytes=60 << 20),
        name="hyena",
    )(jnp.transpose(streams, (1, 0, 2)), long_filter, out_weight, short_filter, skip_gain[None, :], *consts)
    return pl.pallas_call(
        handed_on,
        out_shape=jax.ShapeDtypeStruct((512, 2048), bf16),
        in_specs=[hbm],
        out_specs=hbm,
        scratch_shapes=[pltpu.VMEM((512, 2048), bf16), dma((2, 4))],
        name="handed_on",
    )(result)


def solution(mesh):
    return jax.shard_map(
        body,
        mesh=mesh,
        in_specs=(
            P("ctx", None, "tp"),
            P(None, None, "tp"),
            P("ctx", "tp"),
            P("tp"),
            P("tp", None),
        ),
        out_specs=P("ctx", "tp"),
        check_vma=False,
    )
```
